32 devices in a mesh: grp: 2 (over x), blk: 16 (over z, y, core).
Axes of the slice: x: 2, y: 2, z: 4, core: 2. Of those that a mesh axis runs over, the one named last changes fastest.
Arguments:
- features: bfloat16 [512, 64, 256], P(('grp', 'blk')), parts along dimension 0, may hold values from -6 to 6
- occupancy: int32 [512, 64], P(('grp', 'blk')), parts along dimension 0, may hold values 0 or 1
- neighbors: int32 [512, 6], P(('grp', 'blk')), parts along dimension 0, may hold values from -1 to 15
- previous: bfloat16 [512, 64, 256], P(('grp', 'blk')), parts along dimension 0, may hold values from -6 to 6
- old_owner: int32 [512, 1], P(('grp', 'blk')), parts along dimension 0, may hold values from 0 to 15; in each aligned block of 16 rows (0 to 15, 16 to 31, ...) at most 2 rows name the same one
- old_slot: int32 [512], P(('grp', 'blk')), parts along dimension 0, may hold values from 0 to 15
- conv_weight: bfloat16 [27, 256, 256], replicated, may hold values from -0.078125 to 0.078125
- norm_scale: float32 [256], replicated, may hold values from 0.1 to 1.9
- norm_shift: float32 [256], replicated, may hold values from -3 to 3
- prev_weight: bfloat16 [256, 256], replicated, may hold values from -0.375 to 0.375
Outputs:
- merged: bfloat16 [512, 64, 256], P(('grp', 'blk')), parts along dimension 0
The draws below stay inside these ranges and needn't reach their ends.
There are 2 independent parts, one for each index of `grp`. The reference program is written for one: setup_inputs(seed, part) draws one part's arguments, and reference() takes and returns one part's arrays. A program takes and returns all parts, laid end to end along the dimension named above; an argument that names none is the same for every part. Nothing has to cross between parts.
Inputs may be any that keep to these rules, and one draw needn't show every extreme that they name: `old_owner`: among the 16 block slots of one device, at most 2 name the same old owner.
All inputs are finite; a program needn't handle non-finite values. No bound on the sum of `occupancy` on one device may be relied on, other than what follows from the above.
Results may differ from the reference program's by a relative error of at most 0.0034.
Values may be sent and summed in bfloat16 or wider, within the bound.
No kernel may reach another device: no remote copies, remote signals or barrier semaphores. Data moves between devices by JAX's collectives and lax.ppermute only.
A program may use at most 128 MiB of HBM per device.

```python
import math
import jax
import jax.numpy as jnp
import numpy as np
from jax import lax

C = 256
EDGE = 4
TAPS = 27
B_DEV = 16
CAP = 2
VOX = 64
BLOCKS = 256
N_BLK = 16


def set_ends(values, rng, low, high):
    spot = [jax.random.randint(jax.random.fold_in(rng, axis), (), 0, length) for axis, length in enumerate(values.shape)]
    longest = values.shape.index(max(values.shape))
    next_to = spot[:longest] + [(spot[longest] + 1) % values.shape[longest]] + spot[longest + 1:]
    return values.at[tuple(spot)].set(low).at[tuple(next_to)].set(high)


def block_scale(key, dims, pieces, smallest, top_value):
    loudness, own = 1.0, jax.random.fold_in(key, 6)
    for axis_at, parts in pieces:
        draws = jnp.exp(jax.random.uniform(jax.random.fold_in(own, axis_at), (parts,), jnp.float32, smallest / len(pieces), top_value / len(pieces)))
        loudness = loudness * jnp.repeat(draws, dims[axis_at] // parts).reshape([-1 if axis == axis_at else 1 for axis in range(len(dims))])
    return loudness


def deal_out(rng, own, number, rows, count, top, most, slope):
    ranking = jax.random.permutation(rng, count)
    heavy_load, ordinary = load_shares(count, rows * top, most, slope, True), load_shares(count, rows * top, most, slope, False)
    places = jnp.arange(count)

    def named(sizes, rotation):
        used = int((sizes > 0).sum())
        fixed = max(1, used // 4)
        shifted = fixed + (places - fixed + rotation * (used - fixed)) % max(1, count - fixed)
        return jnp.zeros((count,), jnp.int32).at[ranking[jnp.where(places < fixed, places, shifted)]].set(jnp.asarray(sizes, jnp.int32))

    sizes = jnp.where(number % 4 == 0, named(heavy_load, number // 4), named(ordinary, number - number // 4 - 1))
    mixed = jax.random.permutation(jax.random.fold_in(own, 3), count)
    donor, receiver = mixed[0:count // 2 * 2:2], mixed[1:count // 2 * 2:2]
    room = jnp.minimum(sizes[donor] - 1, most - sizes[receiver]) // 2
    room = jnp.where((donor == ranking[0]) | (receiver == ranking[0]) | (sizes[receiver] == 0), 0, jnp.maximum(room, 0))
    shifted = jax.random.randint(jax.random.fold_in(own, 4), (count // 2,), 0, 1 << 20) % (room + 1)
    sizes = sizes.at[donor].add(-shifted).at[receiver].add(shifted)
    labels = jnp.searchsorted(jnp.cumsum(sizes), jnp.arange(rows * top), side="right").astype(jnp.int32)
    grid = labels.reshape(top, rows).T
    grid = grid[jax.random.permutation(jax.random.fold_in(own, 1), rows)]
    rotation = jax.random.randint(jax.random.fold_in(own, 2), (rows, 1), 0, top)
    return jnp.take_along_axis(grid, (jnp.arange(top)[None, :] + rotation) % top, axis=1)


def load_shares(amount, total, limit, lean, full):
    loads = [(1 << 20) // math.isqrt(rank ** lean) + 1 for rank in range(1, amount + 1)]
    largest = limit if full else min(limit, max(-(-total // amount), total * loads[0] // sum(loads)))
    least = 1 if total - largest >= amount - 1 else 0
    counts, surplus = [largest] + [least] * (amount - 1), total - largest - least * (amount - 1)
    while surplus > 0:
        free = [i for i in range(1, amount) if counts[i] < largest] or [i for i in range(1, amount) if counts[i] < limit]
        whole, remaining = sum([loads[i] for i in free]), surplus
        for i in free:
            more = min(limit - counts[i], max(1, remaining * loads[i] // whole), surplus)
            counts[i] = counts[i] + more
            surplus = surplus - more
    return np.array(counts)


def centred(own_key, dims, width, bound, shards=(), dtype=jnp.bfloat16):
    factor_of = block_scale(own_key, dims, shards, -0.22, 0.18) if shards else 1.0
    result = jax.random.normal(own_key, dims, jnp.float32) * width * factor_of
    return jnp.minimum(jnp.maximum(result, -bound), bound).astype(dtype)


def setup_inputs(seed: int = 0, part: int = 0) -> dict:
    key_of = jax.random.split(jax.random.key(seed), 11)
    own_keys = jax.random.split(jax.random.fold_in(key_of[10], part), 11)
    features = centred(own_keys[0], (BLOCKS, VOX, C), 1.0, 6.0, ((0, 16),))
    occupancy = set_ends((jax.random.randint(own_keys[1], (BLOCKS, VOX), 0, 4) < 3).astype(jnp.int32), jax.random.fold_in(own_keys[1], 1), 0, 1)
    neighbors = set_ends(jax.random.randint(own_keys[2], (BLOCKS, 6), -1, B_DEV), jax.random.fold_in(own_keys[2], 1), -1, B_DEV - 1).astype(jnp.int32)
    previous = centred(own_keys[3], (BLOCKS, VOX, C), 1.0, 6.0, ((0, 16),))
    old_owner_keys = jax.random.split(jax.random.fold_in(own_keys[4], 1), BLOCKS // B_DEV)
    old_owner_turns = jax.random.permutation(jax.random.fold_in(own_keys[4], 3), BLOCKS // B_DEV)
    old_owner = jax.vmap(lambda own, number: deal_out(jax.random.fold_in(own_keys[4], 2), own, number, B_DEV, N_BLK, 1, CAP, 2))(old_owner_keys, old_owner_turns).reshape((BLOCKS, 1))
    old_slot = set_ends(jax.random.randint(own_keys[5], (BLOCKS,), 0, B_DEV), jax.random.fold_in(own_keys[5], 1), 0, B_DEV - 1).astype(jnp.int32)
    conv_weight = centred(key_of[6], (TAPS, C, C), (TAPS * C) ** -0.5, 0.078125)
    norm_scale = jnp.clip(1.0 + 0.18 * jax.random.normal(key_of[7], (C,), jnp.float32), 0.1, 1.9)
    norm_shift = centred(key_of[8], (C,), 0.5, 3.0, (), jnp.float32)
    prev_weight = centred(key_of[9], (C, C), C ** -0.5, 0.375)
    return {"features": features, "occupancy": occupancy, "neighbors": neighbors, "previous": previous, "old_owner": old_owner, "old_slot": old_slot, "conv_weight": conv_weight, "norm_scale": norm_scale, "norm_shift": norm_shift, "prev_weight": prev_weight}


def face_layers(cube, slots, device_shift, layer, axis_pos):
    block_total = cube.shape[0]
    positions = jnp.arange(block_total).astype(jnp.int32)
    owner_dev = positions // B_DEV + device_shift
    valid = (slots >= 0) & (owner_dev >= 0) & (owner_dev < N_BLK)
    source = jnp.clip(owner_dev * B_DEV + slots, 0, block_total - 1).astype(jnp.int32)
    layers = jnp.take(cube, layer, axis=axis_pos)[source]
    return layers * valid.astype(jnp.bfloat16)[:, None, None, None]


def reference(features, occupancy, neighbors, previous, old_owner, old_slot, conv_weight, norm_scale, norm_shift, prev_weight):
    block_total = features.shape[0]
    occ_mask = occupancy.astype(jnp.bfloat16)[:, :, None]
    masked = features * occ_mask
    cube = masked.reshape(block_total, EDGE, EDGE, EDGE, C)
    volume = jnp.zeros((block_total, EDGE + 2, EDGE + 2, EDGE + 2, C), jnp.bfloat16)
    volume = volume.at[:, 1:EDGE + 1, 1:EDGE + 1, 1:EDGE + 1].set(cube)
    volume = volume.at[:, 0, 1:EDGE + 1, 1:EDGE + 1].set(face_layers(cube, neighbors[:, 0], -1, EDGE - 1, 1))
    volume = volume.at[:, EDGE + 1, 1:EDGE + 1, 1:EDGE + 1].set(face_layers(cube, neighbors[:, 1], 1, 0, 1))
    volume = volume.at[:, 1:EDGE + 1, 0, 1:EDGE + 1].set(face_layers(cube, neighbors[:, 2], 0, EDGE - 1, 2))
    volume = volume.at[:, 1:EDGE + 1, EDGE + 1, 1:EDGE + 1].set(face_layers(cube, neighbors[:, 3], 0, 0, 2))
    volume = volume.at[:, 1:EDGE + 1, 1:EDGE + 1, 0].set(face_layers(cube, neighbors[:, 4], 0, EDGE - 1, 3))
    volume = volume.at[:, 1:EDGE + 1, 1:EDGE + 1, EDGE + 1].set(face_layers(cube, neighbors[:, 5], 0, 0, 3))
    conv_out = jnp.zeros((block_total * EDGE * EDGE * EDGE, C), jnp.float32)
    for shift_a in range(3):
        for shift_b in range(3):
            for shift_c in range(3):
                window = volume[:, shift_a:shift_a + EDGE, shift_b:shift_b + EDGE, shift_c:shift_c + EDGE]
                conv_out = conv_out + jnp.dot(window.reshape(-1, C), conv_weight[(3 * shift_a + shift_b) * 3 + shift_c], preferred_element_type=jnp.float32)
    hidden = jnp.maximum(conv_out * norm_scale[None, :] + norm_shift[None, :], 0.0)
    source = (old_owner[:, 0] * B_DEV + old_slot).astype(jnp.int32)
    moved = previous[source]
    projected = jnp.dot(moved.reshape(-1, C), prev_weight, preferred_element_type=jnp.float32).astype(jnp.bfloat16)
    projected = lax.optimization_barrier(projected)
    occ_float = occupancy.astype(jnp.float32).reshape(-1, 1)
    merged = (hidden + projected.astype(jnp.float32)) * occ_float
    return merged.reshape(block_total, EDGE * EDGE * EDGE, C).astype(jnp.bfloat16)
```

```python
import functools

import jax
import jax.numpy as jnp
from jax import lax
from jax.experimental import pallas as pl
from jax.experimental.pallas import tpu as pltpu
from jax.sharding import PartitionSpec as P

EDGE = 4
LAYER = EDGE * EDGE
VOX = EDGE * LAYER
PLANE = 4
LANES = 128
HBM = pl.BlockSpec(memory_space=pl.ANY)
VMEM = pl.BlockSpec(memory_space=pltpu.VMEM)
SMEM = pl.BlockSpec(memory_space=pltpu.SMEM)


def near(array):
    return pltpu.with_memory_space_constraint(array, pltpu.VMEM)


def far(array):
    return pltpu.with_memory_space_constraint(array, pltpu.HBM)


def cost(flops, moved):
    return pl.CostEstimate(flops=flops, bytes_accessed=moved, transcendentals=0)


def occupied(occ, layer, channels):
    slots = occ.shape[0]
    shape = (LAYER, slots, VOX)
    voxel = lax.broadcasted_iota(jnp.int32, shape, 0) + layer * LAYER
    column = lax.broadcasted_iota(jnp.int32, shape, 2)
    picked = jnp.where(voxel == column, jnp.broadcast_to(occ[None], shape), 0.0)
    picked = picked.astype(jnp.bfloat16).reshape(LAYER * slots, VOX)
    ones = jnp.ones((VOX, channels), jnp.bfloat16)
    return jnp.dot(picked, ones, preferred_element_type=jnp.float32)


def params(mib):
    return pltpu.CompilerParams(vmem_limit_bytes=mib * 1024 * 1024)


def start_all(pairs, sems):
    copies = [pltpu.make_async_copy(src, dst, sems.at[i]) for i, (src, dst) in enumerate(pairs)]
    for copy in copies:
        copy.start()
    return copies


def prepare_kernel(
    features, occupancy, previous, after, cube, core, next_, own, values_in, occ_in, sems
):
    slots, _, channels = features.shape
    rows = LAYER * slots
    copies = start_all(((features, values_in), (occupancy, occ_in), (previous, own)), sems)
    row = lax.broadcasted_iota(jnp.int32, (rows, rows), 0)
    column = lax.broadcasted_iota(jnp.int32, (rows, rows), 1)
    swap = (row // slots == column % LAYER) & (row % slots == column // LAYER)
    swap = jnp.where(swap, 1.0, 0.0).astype(jnp.bfloat16)
    even = lax.rem(lax.axis_index("blk"), 2) == 0
    copies[1].wait()
    occ = occ_in[...].astype(jnp.float32)
    copies[0].wait()
    for layer in range(EDGE):
        span = pl.ds(layer * LAYER, LAYER)
        values = values_in[:, span, :].reshape(rows, channels)
        turned = jnp.dot(swap, values, preferred_element_type=jnp.float32)
        turned = turned * occupied(occ, layer, channels)
        cube[span] = turned.astype(jnp.bfloat16).reshape(LAYER, slots, channels)
    first, last = pl.ds(0, LAYER), pl.ds(VOX - LAYER, LAYER)

    @pl.when(even)
    def _():
        core[...] = cube[last]
        next_[...] = cube[first]

    @pl.when(jnp.logical_not(even))
    def _():
        core[...] = cube[first]
        next_[...] = cube[last]

    copies[2].wait()


def conv_kernel(
    cube, core, next_, near_t, occupancy, weight, scale, shift, after, hidden,
    volume, taps, total, near_in, occ_in, scale_in, shift_in, sems,
):
    slots, channels = cube.shape[1], cube.shape[2]
    rows = LAYER * slots
    side = EDGE + 2
    copies = start_all(
        [(near_t, near_in), (occupancy, occ_in), (scale, scale_in), (shift, shift_in)]
        + [(weight.at[pl.ds(9 * a, 9)], taps.at[pl.ds(9 * a, 9)]) for a in range(3)],
        sems,
    )
    even = lax.rem(lax.axis_index("blk"), 2) == 0
    volume[...] = jnp.zeros(volume.shape, volume.dtype)
    inner = pl.ds(1, EDGE)
    cells = cube[...].reshape(EDGE, EDGE, EDGE, slots, channels)
    volume[inner, inner, inner] = cells

    row = lax.broadcasted_iota(jnp.int32, (rows, rows), 0)
    column = lax.broadcasted_iota(jnp.int32, (rows, rows), 1)
    same_place = row // slots == column // slots
    slot_of = (column % slots).astype(jnp.float32)
    spread = lax.broadcasted_iota(jnp.int32, (rows, slots), 0) % slots
    spread = spread == lax.broadcasted_iota(jnp.int32, (rows, slots), 1)
    spread = jnp.where(spread, 1.0, 0.0).astype(jnp.bfloat16)
    for copy in copies[:4]:
        copy.wait()
    near_rows = lax.dot_general(
        spread,
        near_in[...].astype(jnp.float32).astype(jnp.bfloat16),
        (((1,), (1,)), ((), ())),
        preferred_element_type=jnp.float32,
    )

    def gathered(face, layer):
        pick = same_place & (slot_of == near_rows[:, face : face + 1])
        pick = jnp.where(pick, 1.0, 0.0).astype(jnp.bfloat16)
        layer = layer.reshape(rows, channels)
        out = jnp.dot(pick, layer, preferred_element_type=jnp.float32).astype(jnp.bfloat16)
        return out.reshape(EDGE, EDGE, slots, channels)

    @pl.when(even)
    def _():
        volume[0, inner, inner] = gathered(0, next_[...])
        volume[EDGE + 1, inner, inner] = gathered(1, core[...])

    @pl.when(jnp.logical_not(even))
    def _():
        volume[0, inner, inner] = gathered(0, core[...])
        volume[EDGE + 1, inner, inner] = gathered(1, next_[...])

    last = EDGE - 1
    volume[inner, 0, inner] = gathered(2, cells[:, last])
    volume[inner, EDGE + 1, inner] = gathered(3, cells[:, 0])
    volume[inner, inner, 0] = gathered(4, cells[:, :, last])
    volume[inner, inner, EDGE + 1] = gathered(5, cells[:, :, 0])

    occ = occ_in[...].astype(jnp.float32)
    for a in range(3):
        copies[4 + a].wait()
        for x in range(EDGE):
            windows = [
                volume[x + a, pl.ds(b, EDGE), pl.ds(c, EDGE)].reshape(rows, channels)
                for b in range(3)
                for c in range(3)
            ]
            joined = jnp.concatenate(windows, axis=1)
            kernel = taps[pl.ds(9 * a, 9)].reshape(9 * channels, channels)
            part = jnp.dot(joined, kernel, preferred_element_type=jnp.float32)
            span = pl.ds(x * rows, rows)
            if a == 2:
                full = occupied(occ, x, LANES)
            for h in range(channels // LANES):
                lanes = slice(h * LANES, (h + 1) * LANES)
                if a == 0:
                    total[h, span] = part[:, lanes]
                elif a == 1:
                    total[h, span] += part[:, lanes]
                else:
                    out = (total[h, span] + part[:, lanes]) * scale_in[:, lanes] + shift_in[:, lanes]
                    total[h, span] = jnp.where(full > 0.5, jnp.maximum(out, 0.0), -1.0)
    for x in range(EDGE):
        for slot in range(slots):
            for h in range(channels // LANES):
                hidden[slot, pl.ds(x * LAYER, LAYER), pl.ds(h * LANES, LANES)] = total[
                    h, pl.ds(x * rows + slot, LAYER, stride=slots), :
                ]


def ask_kernel(first, second, planes, old_owner, old_slot, *refs):
    steps = planes - 1
    asks, plan = refs[:steps], refs[steps]
    queue, used = refs[steps + 1 :]
    slots = old_slot.shape[0]
    me = lax.axis_index("blk")
    width = first + second

    def clear(i, _):
        queue[i] = 0
        plan[i] = slots
        return 0

    lax.fori_loop(0, planes * width, clear, 0)
    for k in range(planes):
        used[k] = 0
        used[planes + k] = 0

    def place(s, _):
        owner = old_owner[s]
        side = lax.bitwise_and(lax.bitwise_xor(owner, me), PLANE - 1)
        block = side * slots + old_slot[s]
        step = lax.rem(me // PLANE - owner // PLANE + planes, planes)
        n_first, n_second = used[step], used[planes + step]
        early = (side < 2) & (n_first < first)
        at = step * width + jnp.where(early, n_first, first + n_second)
        used[step] = jnp.where(early, n_first + 1, n_first)
        used[planes + step] = jnp.where(early, n_second, n_second + 1)
        queue[at] = block
        plan[at] = s
        return 0

    lax.fori_loop(0, slots, place, 0)
    for i in range(width):
        plan[planes * width + i] = queue[i]
        for k in range(1, planes):
            asks[k - 1][i] = queue[k * width + i]


def pack_kernel(begin, count, steps, pools_n, *refs):
    asks, pools, refs = refs[:steps], refs[steps : steps + pools_n], refs[steps + pools_n :]
    outs, lists, sems = refs[-steps - 2 : -2], refs[-2], refs[-1]
    slots = pools[0].shape[0]
    copies = start_all([(asks[k], lists.at[k]) for k in range(steps)], sems)
    for k in range(steps):
        copies[k].wait()
        for i in range(count):
            block = lists[k, begin + i]
            for p, pool in enumerate(pools):
                @pl.when(block // slots == p)
                def _():
                    outs[k][i] = pool[lax.rem(block, slots)]


def pack(asks, pools, begin, count, after=()):
    block = pools[0].shape[1:]
    dtype = pools[0].dtype
    steps = len(asks)
    return pl.pallas_call(
        functools.partial(pack_kernel, begin, count, steps, len(pools)),
        out_shape=[pltpu.VMEM((count,) + block, dtype)] * steps,
        in_specs=[VMEM] * steps + [VMEM] * len(pools) + [HBM] * len(after),
        out_specs=[VMEM] * steps,
        scratch_shapes=[
            pltpu.SMEM((steps,) + asks[0].shape, jnp.int32),
            pltpu.SemaphoreType.DMA((steps,)),
        ],
        compiler_params=params(1),
        cost_estimate=cost(0, 3000000),
    )(*map(near, asks), *map(near, pools), *after)


def finish_kernel(first, second, steps, plan, hidden, weight, *refs):
    pools = refs[:PLANE]
    early, late = refs[PLANE : PLANE + steps], refs[PLANE + steps : PLANE + 2 * steps]
    out, moved, merged, plan_in, weight_in, sems = refs[PLANE + 2 * steps :]
    slots = out.shape[0]
    width = first + second
    copies = start_all(((plan, plan_in), (weight, weight_in)), sems)
    copies[0].wait()
    for i in range(width):
        block = plan_in[(steps + 1) * width + i]
        for p, pool in enumerate(pools):
            @pl.when(block // slots == p)
            def _():
                moved[plan_in[i]] = pool[lax.rem(block, slots)]
    for k in range(steps):
        at = (k + 1) * width
        for i in range(first):
            moved[plan_in[at + i]] = early[k][i]
        for i in range(second):
            moved[plan_in[at + first + i]] = late[k][i]
    copies[1].wait()
    group = min(4, slots)
    sent = []
    for j, g in enumerate(range(0, slots, group)):
        span = pl.ds(g, group)
        values = moved[span].reshape(group * VOX, moved.shape[2])
        projected = jnp.dot(values, weight_in[...], preferred_element_type=jnp.float32)
        projected = projected.astype(jnp.bfloat16).astype(jnp.float32)
        base = hidden[span].reshape(group * VOX, hidden.shape[2])
        done = jnp.where(base < 0.0, 0.0, base + projected)
        merged[span] = done.astype(out.dtype).reshape(group, VOX, out.shape[2])
        sent.append(pltpu.make_async_copy(merged.at[span], out.at[span], sems.at[2 + j]))
        sent[-1].start()
    for copy in sent:
        copy.wait()


def per_device(
    features,
    occupancy,
    neighbors,
    previous,
    old_owner,
    old_slot,
    conv_weight,
    norm_scale,
    norm_shift,
    prev_weight,
):
    slots, _, channels = features.shape
    rows = LAYER * slots
    count = lax.axis_size("blk")
    planes = count // PLANE
    cap = max(2, 2 * slots // count)
    first, second = 2 * cap, 2 * cap
    steps = planes - 1
    width = first + second

    def beside(array, flip):
        return lax.ppermute(array, "blk", [(i, i ^ flip) for i in range(count)])

    def along(array, step):
        return lax.ppermute(array, "blk", [(i, (i + PLANE * step) % count) for i in range(count)])

    prev_y = beside(previous, 2)
    prev_c = beside(previous, 1)

    ints = lambda *shape: jax.ShapeDtypeStruct(shape, jnp.int32)
    *asks, plan = pl.pallas_call(
        functools.partial(ask_kernel, first, second, planes),
        out_shape=[ints(width)] * steps + [ints((planes + 1) * width)],
        in_specs=[SMEM] * 2,
        out_specs=[SMEM] * (steps + 1),
        scratch_shapes=[pltpu.SMEM((planes * width,), jnp.int32), pltpu.SMEM((2 * planes,), jnp.int32)],
        compiler_params=params(1),
        cost_estimate=cost(0, 2000),
    )(old_owner.reshape(slots), old_slot)
    asked = [along(ask, -k) for k, ask in enumerate(asks, 1)]

    near_block = lambda *shape: pltpu.VMEM(shape, jnp.bfloat16)
    cube, to_core, to_next, own = pl.pallas_call(
        prepare_kernel,
        out_shape=[
            near_block(VOX, slots, channels),
            near_block(LAYER, slots, channels),
            near_block(LAYER, slots, channels),
            near_block(*previous.shape),
        ],
        in_specs=[HBM] * 3 + [HBM],
        out_specs=[VMEM] * 4,
        scratch_shapes=[
            pltpu.VMEM(features.shape, features.dtype),
            pltpu.VMEM(occupancy.shape, occupancy.dtype),
            pltpu.SemaphoreType.DMA((3,)),
        ],
        compiler_params=params(4),
        cost_estimate=cost(2 * EDGE * rows * (rows + VOX) * channels, 5 * rows * channels * 4),
    )(far(features), far(occupancy), far(previous), plan)
    from_core = beside(to_core, 1)
    from_next = lax.ppermute(
        to_next,
        "blk",
        [pair for i in range(1, count - 1, 2) for pair in ((i, i + 1), (i + 1, i))],
    )

    early = pack(asked, [own, prev_c], 0, first)
    sent = [along(part, k) for k, part in enumerate(early, 1)]
    prev_yc = beside(lax.optimization_barrier((prev_y, early[0]))[0], 1)
    pools = [own, prev_c, prev_y, prev_yc]
    late = pack(asked, pools, first, second, [early[0], from_core, from_next])
    sent += [along(part, k) for k, part in enumerate(late, 1)]

    side = EDGE + 2
    hidden = pl.pallas_call(
        conv_kernel,
        out_shape=pltpu.VMEM((slots, VOX, channels), jnp.float32),
        in_specs=[VMEM] * 3 + [HBM] * 6,
        out_specs=VMEM,
        scratch_shapes=[
            pltpu.VMEM((side, side, side, slots, channels), jnp.bfloat16),
            pltpu.VMEM(conv_weight.shape, jnp.bfloat16),
            pltpu.VMEM((channels // LANES, EDGE * rows, LANES), jnp.float32),
            pltpu.VMEM((6, slots), jnp.int32),
            pltpu.VMEM(occupancy.shape, jnp.int32),
            pltpu.VMEM((1, channels), jnp.float32),
            pltpu.VMEM((1, channels), jnp.float32),
            pltpu.SemaphoreType.DMA((7,)),
        ],
        compiler_params=params(12),
        cost_estimate=cost(2 * 27 * EDGE * rows * channels * channels, 8000000),
    )(
        near(cube),
        near(from_core),
        near(from_next),
        far(neighbors.T),
        far(occupancy),
        far(conv_weight),
        far(norm_scale[None]),
        far(norm_shift[None]),
        late[0],
    )

    return pl.pallas_call(
        functools.partial(finish_kernel, first, second, steps),
        out_shape=jax.ShapeDtypeStruct((slots, VOX, channels), jnp.bfloat16),
        in_specs=[HBM, VMEM, HBM] + [VMEM] * (PLANE + 2 * steps),
        out_specs=HBM,
        scratch_shapes=[
            near_block(slots + 1, VOX, channels),
            near_block(slots, VOX, channels),
            pltpu.SMEM(((planes + 1) * width,), jnp.int32),
            near_block(channels, channels),
            pltpu.SemaphoreType.DMA((2 + -(-slots // 4),)),
        ],
        compiler_params=params(4),
        cost_estimate=cost(2 * VOX * slots * channels * channels, 3000000),
    )(far(plan), near(hidden), far(prev_weight), *map(near, (*pools, *sent)))


def solution(mesh):
    rows = ("grp", "blk")
    in_specs = (
        P(rows, None, None),
        P(rows, None),
        P(rows, None),
        P(rows, None, None),
        P(rows, None),
        P(rows),
        P(),
        P(),
        P(),
        P(),
    )
    return jax.shard_map(
        per_device, mesh=mesh, in_specs=in_specs, out_specs=P(rows, None, None), check_vma=False
    )
```

```python
import functools

import jax
import jax.numpy as jnp
from jax import lax
from jax.experimental import pallas as pl
from jax.experimental.pallas import tpu as pltpu
from jax.sharding import PartitionSpec as P

EDGE = 4
LAYER = EDGE * EDGE
VOX = EDGE * LAYER
PLANE = 4
LANES = 128
HBM = pl.BlockSpec(memory_space=pl.ANY)
VMEM = pl.BlockSpec(memory_space=pltpu.VMEM)
SMEM = pl.BlockSpec(memory_space=pltpu.SMEM)


def near(array):
    return pltpu.with_memory_space_constraint(array, pltpu.VMEM)


def far(array):
    return pltpu.with_memory_space_constraint(array, pltpu.HBM)


def cost(flops, moved):
    return pl.CostEstimate(flops=flops, bytes_accessed=moved, transcendentals=0)


def occupied(occ, layer, channels):
    slots = occ.shape[0]
    shape = (LAYER, slots, VOX)
    voxel = lax.broadcasted_iota(jnp.int32, shape, 0) + layer * LAYER
    column = lax.broadcasted_iota(jnp.int32, shape, 2)
    picked = jnp.where(voxel == column, jnp.broadcast_to(occ[None], shape), 0.0)
    picked = picked.astype(jnp.bfloat16).reshape(LAYER * slots, VOX)
    ones = jnp.ones((VOX, channels), jnp.bfloat16)
    return jnp.dot(picked, ones, preferred_element_type=jnp.float32)


def params(mib):
    return pltpu.CompilerParams(vmem_limit_bytes=mib * 1024 * 1024)


def start_all(pairs, sems):
    copies = [pltpu.make_async_copy(src, dst, sems.at[i]) for i, (src, dst) in enumerate(pairs)]
    for copy in copies:
        copy.start()
    return copies


def prepare_kernel(
    features, occupancy, previous, after, after2, cube, core, next_, own, values_in, occ_in, sems
):
    slots, _, channels = features.shape
    rows = LAYER * slots
    copies = start_all(((features, values_in), (occupancy, occ_in), (previous, own)), sems)
    row = lax.broadcasted_iota(jnp.int32, (rows, rows), 0)
    column = lax.broadcasted_iota(jnp.int32, (rows, rows), 1)
    swap = (row // slots == column % LAYER) & (row % slots == column // LAYER)
    swap = jnp.where(swap, 1.0, 0.0).astype(jnp.bfloat16)
    even = lax.rem(lax.axis_index("blk"), 2) == 0
    copies[1].wait()
    occ = occ_in[...].astype(jnp.float32)
    copies[0].wait()
    for layer in range(EDGE):
        span = pl.ds(layer * LAYER, LAYER)
        values = values_in[:, span, :].reshape(rows, channels)
        turned = jnp.dot(swap, values, preferred_element_type=jnp.float32)
        turned = turned * occupied(occ, layer, channels)
        cube[span] = turned.astype(jnp.bfloat16).reshape(LAYER, slots, channels)
    first, last = pl.ds(0, LAYER), pl.ds(VOX - LAYER, LAYER)

    @pl.when(even)
    def _():
        core[...] = cube[last]
        next_[...] = cube[first]

    @pl.when(jnp.logical_not(even))
    def _():
        core[...] = cube[first]
        next_[...] = cube[last]

    copies[2].wait()


def conv_kernel(
    room, steps, cube, core, next_, own, other, near_t, occupancy, weight, scale, shift, plan, after, *refs
):
    early = refs[:steps]
    hidden, moved, volume, taps, total, near_in, occ_in, scale_in, shift_in, plan_in, sems = refs[steps:]
    slots, channels = cube.shape[1], cube.shape[2]
    rows = LAYER * slots
    side = EDGE + 2
    copies = start_all(
        [(near_t, near_in), (occupancy, occ_in), (scale, scale_in), (shift, shift_in), (plan, plan_in)]
        + [(weight.at[pl.ds(9 * a, 9)], taps.at[pl.ds(9 * a, 9)]) for a in range(3)],
        sems,
    )
    even = lax.rem(lax.axis_index("blk"), 2) == 0
    volume[...] = jnp.zeros(volume.shape, volume.dtype)
    inner = pl.ds(1, EDGE)
    cells = cube[...].reshape(EDGE, EDGE, EDGE, slots, channels)
    volume[inner, inner, inner] = cells

    row = lax.broadcasted_iota(jnp.int32, (rows, rows), 0)
    column = lax.broadcasted_iota(jnp.int32, (rows, rows), 1)
    same_place = row // slots == column // slots
    slot_of = (column % slots).astype(jnp.float32)
    spread = lax.broadcasted_iota(jnp.int32, (rows, slots), 0) % slots
    spread = spread == lax.broadcasted_iota(jnp.int32, (rows, slots), 1)
    spread = jnp.where(spread, 1.0, 0.0).astype(jnp.bfloat16)
    for copy in copies[:5]:
        copy.wait()
    near_rows = lax.dot_general(
        spread,
        near_in[...].astype(jnp.float32).astype(jnp.bfloat16),
        (((1,), (1,)), ((), ())),
        preferred_element_type=jnp.float32,
    )

    for i in range(room):
        fill(moved.at[plan_in[i]], own, other, plan_in[2 * (steps + 1) * room + i])
        for k in range(steps):
            moved[plan_in[2 * (k + 1) * room + i]] = early[k][i]

    def gathered(face, layer):
        pick = same_place & (slot_of == near_rows[:, face : face + 1])
        pick = jnp.where(pick, 1.0, 0.0).astype(jnp.bfloat16)
        layer = layer.reshape(rows, channels)
        out = jnp.dot(pick, layer, preferred_element_type=jnp.float32).astype(jnp.bfloat16)
        return out.reshape(EDGE, EDGE, slots, channels)

    @pl.when(even)
    def _():
        volume[0, inner, inner] = gathered(0, next_[...])
        volume[EDGE + 1, inner, inner] = gathered(1, core[...])

    @pl.when(jnp.logical_not(even))
    def _():
        volume[0, inner, inner] = gathered(0, core[...])
        volume[EDGE + 1, inner, inner] = gathered(1, next_[...])

    last = EDGE - 1
    volume[inner, 0, inner] = gathered(2, cells[:, last])
    volume[inner, EDGE + 1, inner] = gathered(3, cells[:, 0])
    volume[inner, inner, 0] = gathered(4, cells[:, :, last])
    volume[inner, inner, EDGE + 1] = gathered(5, cells[:, :, 0])

    occ = occ_in[...].astype(jnp.float32)
    for a in range(3):
        copies[5 + a].wait()
        for x in range(EDGE):
            windows = [
                volume[x + a, pl.ds(b, EDGE), pl.ds(c, EDGE)].reshape(rows, channels)
                for b in range(3)
                for c in range(3)
            ]
            joined = jnp.concatenate(windows, axis=1)
            kernel = taps[pl.ds(9 * a, 9)].reshape(9 * channels, channels)
            part = jnp.dot(joined, kernel, preferred_element_type=jnp.float32)
            span = pl.ds(x * rows, rows)
            if a == 2:
                full = occupied(occ, x, LANES)
            for h in range(channels // LANES):
                lanes = slice(h * LANES, (h + 1) * LANES)
                if a == 0:
                    total[h, span] = part[:, lanes]
                elif a == 1:
                    total[h, span] += part[:, lanes]
                else:
                    out = (total[h, span] + part[:, lanes]) * scale_in[:, lanes] + shift_in[:, lanes]
                    total[h, span] = jnp.where(full > 0.5, jnp.maximum(out, 0.0), -1.0)
    for x in range(EDGE):
        for slot in range(slots):
            for h in range(channels // LANES):
                hidden[slot, pl.ds(x * LAYER, LAYER), pl.ds(h * LANES, LANES)] = total[
                    h, pl.ds(x * rows + slot, LAYER, stride=slots), :
                ]


def ask_kernel(room, planes, owner_in, slot_in, *refs):
    steps = planes - 1
    asks, plan = refs[:steps], refs[steps]
    old_owner, old_slot, queue, used, sems = refs[steps + 1 :]
    slots = old_slot.shape[0]
    width = 2 * room
    copies = start_all(((owner_in, old_owner), (slot_in, old_slot)), sems)
    me = lax.axis_index("blk")

    def clear(i, _):
        queue[i] = 0
        plan[i] = slots
        return 0

    lax.fori_loop(0, planes * width, clear, 0)
    for k in range(2 * planes):
        used[k] = 0
    for copy in copies:
        copy.wait()

    def place(s, _):
        away = lax.bitwise_xor(old_owner[s], me)
        chip = away // 2
        n = used[chip]
        used[chip] = n + 1
        at = chip * room + n
        queue[at] = lax.bitwise_and(away, 1) * slots + old_slot[s]
        plan[at] = s
        return 0

    lax.fori_loop(0, slots, place, 0)
    for i in range(width):
        plan[planes * width + i] = queue[i]
        for k in range(1, planes):
            asks[k - 1][i] = queue[k * width + i]


def fill(out, own, other, block):
    slots = own.shape[0]

    @pl.when(block < slots)
    def _():
        out[...] = own[block]

    @pl.when(block >= slots)
    def _():
        out[...] = other[block - slots]


def same_kernel(room, steps, plan, own, other, *refs):
    asks, outs = refs[:steps], refs[steps : 2 * steps]
    lists, asks_in, plan_in, sems = refs[2 * steps :]
    copies = start_all([(asks[k], asks_in.at[k]) for k in range(steps)] + [(plan, plan_in)], sems)
    for k in range(steps):
        copies[k].wait()
        for i in range(room):
            fill(outs[k].at[i], own, other, asks_in[k, i])
            lists[(k + 1) * room + i] = asks_in[k, room + i]
    copies[steps].wait()
    for i in range(room):
        lists[i] = plan_in[2 * (steps + 1) * room + room + i]


def cross_kernel(room, planes, lists, own, other, after, *refs):
    outs, lists_in, sems = refs[:planes], *refs[planes:]
    copies = start_all(((lists, lists_in),), sems)
    copies[0].wait()
    for k in range(planes):
        for i in range(room):
            fill(outs[k].at[i], own, other, lists_in[k * room + i])


def finish_kernel(room, planes, plan, hidden, weight, gathered, *refs):
    cross = refs[:planes]
    out, moved, merged, plan_in, weight_in, sems = refs[planes:]
    slots = out.shape[0]
    copies = start_all(((plan, plan_in), (weight, weight_in)), sems)
    copies[0].wait()
    for k in range(planes):
        for i in range(room):
            moved[plan_in[(2 * k + 1) * room + i]] = cross[k][i]
    copies[1].wait()
    group = min(4, slots)
    sent = []
    for j, g in enumerate(range(0, slots, group)):
        span = pl.ds(g, group)
        values = moved[span].reshape(group * VOX, moved.shape[2])
        projected = jnp.dot(values, weight_in[...], preferred_element_type=jnp.float32)
        projected = projected.astype(jnp.bfloat16).astype(jnp.float32)
        base = hidden[span].reshape(group * VOX, hidden.shape[2])
        done = jnp.where(base < 0.0, 0.0, base + projected)
        merged[span] = done.astype(out.dtype).reshape(group, VOX, out.shape[2])
        sent.append(pltpu.make_async_copy(merged.at[span], out.at[span], sems.at[2 + j]))
        sent[-1].start()
    for copy in sent:
        copy.wait()


def per_device(
    features,
    occupancy,
    neighbors,
    previous,
    old_owner,
    old_slot,
    conv_weight,
    norm_scale,
    norm_shift,
    prev_weight,
):
    slots, _, channels = features.shape
    rows = LAYER * slots
    count = lax.axis_size("blk")
    planes = count // PLANE
    steps = planes - 1
    room = 2 * max(2, 2 * slots // count)
    width = 2 * room

    def swap(array, flip):
        return lax.ppermute(array, "blk", [(i, i ^ flip) for i in range(count)])

    def ints(*shape):
        return jax.ShapeDtypeStruct(shape, jnp.int32)

    def blocks(*shape):
        return pltpu.VMEM(shape, jnp.bfloat16)

    other = swap(previous, 1)

    *asks, plan = pl.pallas_call(
        functools.partial(ask_kernel, room, planes),
        out_shape=[ints(width)] * steps + [ints((planes + 1) * width)],
        in_specs=[HBM] * 2,
        out_specs=[SMEM] * (steps + 1),
        scratch_shapes=[
            pltpu.SMEM((slots,), jnp.int32),
            pltpu.SMEM((slots,), jnp.int32),
            pltpu.SMEM((planes * width,), jnp.int32),
            pltpu.SMEM((2 * planes,), jnp.int32),
            pltpu.SemaphoreType.DMA((2,)),
        ],
        compiler_params=params(1),
        cost_estimate=cost(0, 1000),
    )(far(old_owner.reshape(slots)), far(old_slot))
    asked = [swap(ask, PLANE * k) for k, ask in enumerate(asks, 1)]

    cube, to_core, to_next, own = pl.pallas_call(
        prepare_kernel,
        out_shape=[
            blocks(VOX, slots, channels),
            blocks(LAYER, slots, channels),
            blocks(LAYER, slots, channels),
            blocks(*previous.shape),
        ],
        in_specs=[HBM] * 5,
        out_specs=[VMEM] * 4,
        scratch_shapes=[
            pltpu.VMEM(features.shape, features.dtype),
            pltpu.VMEM(occupancy.shape, occupancy.dtype),
            pltpu.SemaphoreType.DMA((3,)),
        ],
        compiler_params=params(4),
        cost_estimate=cost(0, 1000),
    )(far(features), far(occupancy), far(previous), plan, other)
    from_core = swap(to_core, 1)
    from_next = lax.ppermute(
        to_next,
        "blk",
        [pair for i in range(1, count - 1, 2) for pair in ((i, i + 1), (i + 1, i))],
    )

    *parts, lists = pl.pallas_call(
        functools.partial(same_kernel, room, steps),
        out_shape=[blocks(room, VOX, channels)] * steps + [ints(planes * room)],
        in_specs=[HBM] + [VMEM] * (2 + steps),
        out_specs=[VMEM] * steps + [SMEM],
        scratch_shapes=[
            pltpu.SMEM((steps, width), jnp.int32),
            pltpu.SMEM(plan.shape, jnp.int32),
            pltpu.SemaphoreType.DMA((steps + 1,)),
        ],
        compiler_params=params(1),
        cost_estimate=cost(0, 1000),
    )(far(plan), *map(near, (own, other, *asked)))
    early = [swap(part, PLANE * k) for k, part in enumerate(parts, 1)]
    lists = swap(lists, 2)

    parts = pl.pallas_call(
        functools.partial(cross_kernel, room, planes),
        out_shape=[blocks(room, VOX, channels)] * planes,
        in_specs=[HBM] + [VMEM] * 2 + [HBM],
        out_specs=[VMEM] * planes,
        scratch_shapes=[pltpu.SMEM((planes * room,), jnp.int32), pltpu.SemaphoreType.DMA((1,))],
        compiler_params=params(1),
        cost_estimate=cost(0, 1000),
    )(far(lists), near(own), near(other), from_next)
    late = [swap(part, PLANE * k + 2) for k, part in enumerate(parts)]

    side = EDGE + 2
    hidden, moved = pl.pallas_call(
        functools.partial(conv_kernel, room, steps),
        out_shape=[
            pltpu.VMEM((slots, VOX, channels), jnp.float32),
            blocks(slots + 1, VOX, channels),
        ],
        in_specs=[VMEM] * 5 + [HBM] * 7 + [VMEM] * steps,
        out_specs=[VMEM] * 2,
        scratch_shapes=[
            pltpu.VMEM((side, side, side, slots, channels), jnp.bfloat16),
            pltpu.VMEM(conv_weight.shape, jnp.bfloat16),
            pltpu.VMEM((channels // LANES, EDGE * rows, LANES), jnp.float32),
            pltpu.VMEM((6, slots), jnp.int32),
            pltpu.VMEM(occupancy.shape, jnp.int32),
            pltpu.VMEM((1, channels), jnp.float32),
            pltpu.VMEM((1, channels), jnp.float32),
            pltpu.SMEM(plan.shape, jnp.int32),
            pltpu.SemaphoreType.DMA((8,)),
        ],
        compiler_params=params(12),
        cost_estimate=cost(0, 1000),
    )(
        near(cube),
        near(from_core),
        near(from_next),
        *map(near, (own, other)),
        far(neighbors.T),
        far(occupancy),
        far(conv_weight),
        far(norm_scale[None]),
        far(norm_shift[None]),
        far(plan),
        parts[0],
        *map(near, early),
    )

    return pl.pallas_call(
        functools.partial(finish_kernel, room, planes),
        out_shape=[
            jax.ShapeDtypeStruct((slots, VOX, channels), jnp.bfloat16),
            blocks(slots + 1, VOX, channels),
        ],
        in_specs=[HBM, VMEM, HBM, VMEM] + [VMEM] * planes,
        out_specs=[HBM, VMEM],
        input_output_aliases={3: 1},
        scratch_shapes=[
            blocks(slots, VOX, channels),
            pltpu.SMEM(plan.shape, jnp.int32),
            blocks(channels, channels),
            pltpu.SemaphoreType.DMA((2 + -(-slots // 4),)),
        ],
        compiler_params=params(4),
        cost_estimate=cost(0, 1000),
    )(far(plan), near(hidden), far(prev_weight), near(moved), *map(near, late))[0]


def solution(mesh):
    rows = ("grp", "blk")
    in_specs = (
        P(rows, None, None),
        P(rows, None),
        P(rows, None),
        P(rows, None, None),
        P(rows, None),
        P(rows),
        P(),
        P(),
        P(),
        P(),
    )
    return jax.shard_map(
        per_device, mesh=mesh, in_specs=in_specs, out_specs=P(rows, None, None), check_vma=False
    )
```

```python
import functools

import jax
import jax.numpy as jnp
from jax import lax
from jax.experimental import pallas as pl
from jax.experimental.pallas import tpu as pltpu
from jax.sharding import PartitionSpec as P

EDGE = 4
LAYER = EDGE * EDGE
VOX = EDGE * LAYER
PLANE = 4
LANES = 128
HBM = pl.BlockSpec(memory_space=pl.ANY)
VMEM = pl.BlockSpec(memory_space=pltpu.VMEM)
SMEM = pl.BlockSpec(memory_space=pltpu.SMEM)


def near(array):
    return pltpu.with_memory_space_constraint(array, pltpu.VMEM)


def far(array):
    return pltpu.with_memory_space_constraint(array, pltpu.HBM)


def cost(flops, moved):
    return pl.CostEstimate(flops=flops, bytes_accessed=moved, transcendentals=0)


def occupied(occ, layer, channels):
    slots = occ.shape[0]
    shape = (LAYER, slots, VOX)
    voxel = lax.broadcasted_iota(jnp.int32, shape, 0) + layer * LAYER
    column = lax.broadcasted_iota(jnp.int32, shape, 2)
    picked = jnp.where(voxel == column, jnp.broadcast_to(occ[None], shape), 0.0)
    picked = picked.astype(jnp.bfloat16).reshape(LAYER * slots, VOX)
    ones = jnp.ones((VOX, channels), jnp.bfloat16)
    return jnp.dot(picked, ones, preferred_element_type=jnp.float32)


def params(mib):
    return pltpu.CompilerParams(vmem_limit_bytes=mib * 1024 * 1024)


def start_all(pairs, sems):
    copies = [pltpu.make_async_copy(src, dst, sems.at[i]) for i, (src, dst) in enumerate(pairs)]
    for copy in copies:
        copy.start()
    return copies


def prepare_kernel(
    features, occupancy, previous, prev_weight, after, after2,
    cube, core, next_, own, prev_taps, values_in, occ_in, sems,
):
    slots, _, channels = features.shape
    rows = LAYER * slots
    copies = start_all(((features, values_in), (occupancy, occ_in), (previous, own), (prev_weight, prev_taps)), sems)
    row = lax.broadcasted_iota(jnp.int32, (rows, rows), 0)
    column = lax.broadcasted_iota(jnp.int32, (rows, rows), 1)
    swap = (row // slots == column % LAYER) & (row % slots == column // LAYER)
    swap = jnp.where(swap, 1.0, 0.0).astype(jnp.bfloat16)
    even = lax.rem(lax.axis_index("blk"), 2) == 0
    copies[1].wait()
    occ = occ_in[...].astype(jnp.float32)
    copies[0].wait()
    for layer in range(EDGE):
        span = pl.ds(layer * LAYER, LAYER)
        values = values_in[:, span, :].reshape(rows, channels)
        turned = jnp.dot(swap, values, preferred_element_type=jnp.float32)
        turned = turned * occupied(occ, layer, channels)
        cube[span] = turned.astype(jnp.bfloat16).reshape(LAYER, slots, channels)
    first, last = pl.ds(0, LAYER), pl.ds(VOX - LAYER, LAYER)

    @pl.when(even)
    def _():
        core[...] = cube[last]
        next_[...] = cube[first]

    @pl.when(jnp.logical_not(even))
    def _():
        core[...] = cube[first]
        next_[...] = cube[last]

    copies[2].wait()
    copies[3].wait()


def conv_kernel(
    room, steps, cube, core, next_, own, other, near_t, occupancy, weight, scale, shift, plan, after, *refs
):
    early = refs[:steps]
    hidden, moved, volume, taps, total, near_in, occ_in, scale_in, shift_in, plan_in, sems = refs[steps:]
    slots, channels = cube.shape[1], cube.shape[2]
    rows = LAYER * slots
    side = EDGE + 2
    copies = start_all(
        [(near_t, near_in), (occupancy, occ_in), (scale, scale_in), (shift, shift_in), (plan, plan_in)]
        + [(weight.at[pl.ds(9 * a, 9)], taps.at[pl.ds(9 * a, 9)]) for a in range(3)],
        sems,
    )
    even = lax.rem(lax.axis_index("blk"), 2) == 0
    volume[...] = jnp.zeros(volume.shape, volume.dtype)
    inner = pl.ds(1, EDGE)
    cells = cube[...].reshape(EDGE, EDGE, EDGE, slots, channels)
    volume[inner, inner, inner] = cells

    row = lax.broadcasted_iota(jnp.int32, (rows, rows), 0)
    column = lax.broadcasted_iota(jnp.int32, (rows, rows), 1)
    same_place = row // slots == column // slots
    slot_of = (column % slots).astype(jnp.float32)
    spread = lax.broadcasted_iota(jnp.int32, (rows, slots), 0) % slots
    spread = spread == lax.broadcasted_iota(jnp.int32, (rows, slots), 1)
    spread = jnp.where(spread, 1.0, 0.0).astype(jnp.bfloat16)
    for copy in copies[:5]:
        copy.wait()
    near_rows = lax.dot_general(
        spread,
        near_in[...].astype(jnp.float32).astype(jnp.bfloat16),
        (((1,), (1,)), ((), ())),
        preferred_element_type=jnp.float32,
    )

    for i in range(room):
        fill(moved.at[plan_in[i]], own, other, plan_in[2 * (steps + 1) * room + i])
        for k in range(steps):
            moved[plan_in[2 * (k + 1) * room + i]] = early[k][i]

    def gathered(face, layer):
        pick = same_place & (slot_of == near_rows[:, face : face + 1])
        pick = jnp.where(pick, 1.0, 0.0).astype(jnp.bfloat16)
        layer = layer.reshape(rows, channels)
        out = jnp.dot(pick, layer, preferred_element_type=jnp.float32).astype(jnp.bfloat16)
        return out.reshape(EDGE, EDGE, slots, channels)

    @pl.when(even)
    def _():
        volume[0, inner, inner] = gathered(0, next_[...])
        volume[EDGE + 1, inner, inner] = gathered(1, core[...])

    @pl.when(jnp.logical_not(even))
    def _():
        volume[0, inner, inner] = gathered(0, core[...])
        volume[EDGE + 1, inner, inner] = gathered(1, next_[...])

    last = EDGE - 1
    volume[inner, 0, inner] = gathered(2, cells[:, last])
    volume[inner, EDGE + 1, inner] = gathered(3, cells[:, 0])
    volume[inner, inner, 0] = gathered(4, cells[:, :, last])
    volume[inner, inner, EDGE + 1] = gathered(5, cells[:, :, 0])

    occ = occ_in[...].astype(jnp.float32)
    for a in range(3):
        copies[5 + a].wait()
        for x in range(EDGE):
            windows = [
                volume[x + a, pl.ds(b, EDGE), pl.ds(c, EDGE)].reshape(rows, channels)
                for b in range(3)
                for c in range(3)
            ]
            joined = jnp.concatenate(windows, axis=1)
            kernel = taps[pl.ds(9 * a, 9)].reshape(9 * channels, channels)
            part = jnp.dot(joined, kernel, preferred_element_type=jnp.float32)
            span = pl.ds(x * rows, rows)
            if a == 2:
                full = occupied(occ, x, LANES)
            for h in range(channels // LANES):
                lanes = slice(h * LANES, (h + 1) * LANES)
                if a == 0:
                    total[h, span] = part[:, lanes]
                elif a == 1:
                    total[h, span] += part[:, lanes]
                else:
                    out = (total[h, span] + part[:, lanes]) * scale_in[:, lanes] + shift_in[:, lanes]
                    total[h, span] = jnp.where(full > 0.5, jnp.maximum(out, 0.0), -1.0)
    for x in range(EDGE):
        for slot in range(slots):
            for h in range(channels // LANES):
                hidden[slot, pl.ds(x * LAYER, LAYER), pl.ds(h * LANES, LANES)] = total[
                    h, pl.ds(x * rows + slot, LAYER, stride=slots), :
                ]


def ask_kernel(room, planes, owner_in, slot_in, *refs):
    steps = planes - 1
    asks, plan = refs[:steps], refs[steps]
    old_owner, old_slot, queue, used, sems = refs[steps + 1 :]
    slots = old_slot.shape[0]
    width = 2 * room
    copies = start_all(((owner_in, old_owner), (slot_in, old_slot)), sems)
    me = lax.axis_index("blk")

    def clear(i, _):
        queue[i] = 0
        plan[i] = slots
        return 0

    lax.fori_loop(0, planes * width, clear, 0)
    for k in range(2 * planes):
        used[k] = 0
    for copy in copies:
        copy.wait()

    def place(s, _):
        away = lax.bitwise_xor(old_owner[s], me)
        chip = away // 2
        n = used[chip]
        used[chip] = n + 1
        at = chip * room + n
        queue[at] = lax.bitwise_and(away, 1) * slots + old_slot[s]
        plan[at] = s
        return 0

    lax.fori_loop(0, slots, place, 0)
    for i in range(width):
        plan[planes * width + i] = queue[i]
        for k in range(1, planes):
            asks[k - 1][i] = queue[k * width + i]


def fill(out, own, other, block):
    slots = own.shape[0]

    @pl.when(block < slots)
    def _():
        out[...] = own[block]

    @pl.when(block >= slots)
    def _():
        out[...] = other[block - slots]


def same_kernel(room, steps, plan, own, other, *refs):
    asks, outs = refs[:steps], refs[steps : 2 * steps]
    lists, asks_in, plan_in, sems = refs[2 * steps :]
    copies = start_all([(asks[k], asks_in.at[k]) for k in range(steps)] + [(plan, plan_in)], sems)
    for k in range(steps):
        copies[k].wait()
        for i in range(room):
            fill(outs[k].at[i], own, other, asks_in[k, i])
            lists[(k + 1) * room + i] = asks_in[k, room + i]
    copies[steps].wait()
    for i in range(room):
        lists[i] = plan_in[2 * (steps + 1) * room + room + i]


def cross_kernel(room, planes, lists, own, other, after, *refs):
    outs, lists_in, sems = refs[:planes], *refs[planes:]
    copies = start_all(((lists, lists_in),), sems)
    copies[0].wait()
    for k in range(planes):
        for i in range(room):
            fill(outs[k].at[i], own, other, lists_in[k * room + i])


def finish_kernel(room, planes, plan, hidden, weight_in, gathered, *refs):
    cross = refs[:planes]
    out, moved, merged, plan_in, sems = refs[planes:]
    slots = out.shape[0]
    copies = start_all(((plan, plan_in),), sems)
    copies[0].wait()
    for k in range(planes):
        for i in range(room):
            moved[plan_in[(2 * k + 1) * room + i]] = cross[k][i]
    group = min(4, slots)
    sent = []
    for j, g in enumerate(range(0, slots, group)):
        span = pl.ds(g, group)
        values = moved[span].reshape(group * VOX, moved.shape[2])
        projected = jnp.dot(values, weight_in[...], preferred_element_type=jnp.float32)
        projected = projected.astype(jnp.bfloat16).astype(jnp.float32)
        base = hidden[span].reshape(group * VOX, hidden.shape[2])
        done = jnp.where(base < 0.0, 0.0, base + projected)
        merged[span] = done.astype(out.dtype).reshape(group, VOX, out.shape[2])
        sent.append(pltpu.make_async_copy(merged.at[span], out.at[span], sems.at[1 + j]))
        sent[-1].start()
    for copy in sent:
        copy.wait()


def per_device(
    features,
    occupancy,
    neighbors,
    previous,
    old_owner,
    old_slot,
    conv_weight,
    norm_scale,
    norm_shift,
    prev_weight,
):
    slots, _, channels = features.shape
    rows = LAYER * slots
    count = lax.axis_size("blk")
    planes = count // PLANE
    steps = planes - 1
    room = 2 * max(2, 2 * slots // count)
    width = 2 * room

    def swap(array, flip):
        return lax.ppermute(array, "blk", [(i, i ^ flip) for i in range(count)])

    def ints(*shape):
        return jax.ShapeDtypeStruct(shape, jnp.int32)

    def blocks(*shape):
        return pltpu.VMEM(shape, jnp.bfloat16)

    other = swap(previous, 1)

    *asks, plan = pl.pallas_call(
        functools.partial(ask_kernel, room, planes),
        out_shape=[ints(width)] * steps + [ints((planes + 1) * width)],
        in_specs=[HBM] * 2,
        out_specs=[SMEM] * (steps + 1),
        scratch_shapes=[
            pltpu.SMEM((slots,), jnp.int32),
            pltpu.SMEM((slots,), jnp.int32),
            pltpu.SMEM((planes * width,), jnp.int32),
            pltpu.SMEM((2 * planes,), jnp.int32),
            pltpu.SemaphoreType.DMA((2,)),
        ],
        compiler_params=params(1),
        cost_estimate=cost(0, 1000),
    )(far(old_owner.reshape(slots)), far(old_slot))
    asked = [swap(ask, PLANE * k) for k, ask in enumerate(asks, 1)]

    cube, to_core, to_next, own, prev_taps = pl.pallas_call(
        prepare_kernel,
        out_shape=[
            blocks(VOX, slots, channels),
            blocks(LAYER, slots, channels),
            blocks(LAYER, slots, channels),
            blocks(*previous.shape),
            blocks(*prev_weight.shape),
        ],
        in_specs=[HBM] * 6,
        out_specs=[VMEM] * 5,
        scratch_shapes=[
            pltpu.VMEM(features.shape, features.dtype),
            pltpu.VMEM(occupancy.shape, occupancy.dtype),
            pltpu.SemaphoreType.DMA((4,)),
        ],
        compiler_params=params(4),
        cost_estimate=cost(0, 1000),
    )(far(features), far(occupancy), far(previous), far(prev_weight), plan, other)
    from_core = swap(to_core, 1)
    from_next = lax.ppermute(
        to_next,
        "blk",
        [pair for i in range(1, count - 1, 2) for pair in ((i, i + 1), (i + 1, i))],
    )

    *parts, lists = pl.pallas_call(
        functools.partial(same_kernel, room, steps),
        out_shape=[blocks(room, VOX, channels)] * steps + [ints(planes * room)],
        in_specs=[HBM] + [VMEM] * (2 + steps),
        out_specs=[VMEM] * steps + [SMEM],
        scratch_shapes=[
            pltpu.SMEM((steps, width), jnp.int32),
            pltpu.SMEM(plan.shape, jnp.int32),
            pltpu.SemaphoreType.DMA((steps + 1,)),
        ],
        compiler_params=params(1),
        cost_estimate=cost(0, 1000),
    )(far(plan), *map(near, (own, other, *asked)))
    early = {k: swap(parts[k - 1], PLANE * k) for k in sorted(range(1, planes), key=lambda k: k < 2)}
    early = [early[k] for k in range(1, planes)]
    lists = swap(lists, 2)

    parts = pl.pallas_call(
        functools.partial(cross_kernel, room, planes),
        out_shape=[blocks(room, VOX, channels)] * planes,
        in_specs=[HBM] + [VMEM] * 2 + [HBM],
        out_specs=[VMEM] * planes,
        scratch_shapes=[pltpu.SMEM((planes * room,), jnp.int32), pltpu.SemaphoreType.DMA((1,))],
        compiler_params=params(1),
        cost_estimate=cost(0, 1000),
    )(far(lists), near(own), near(other), from_next)
    late = {k: swap(parts[k], PLANE * k + 2) for k in sorted(range(planes), key=lambda k: k < 2)}
    late = [late[k] for k in range(planes)]

    side = EDGE + 2
    hidden, moved = pl.pallas_call(
        functools.partial(conv_kernel, room, steps),
        out_shape=[
            pltpu.VMEM((slots, VOX, channels), jnp.float32),
            blocks(slots + 1, VOX, channels),
        ],
        in_specs=[VMEM] * 5 + [HBM] * 7 + [VMEM] * steps,
        out_specs=[VMEM] * 2,
        scratch_shapes=[
            pltpu.VMEM((side, side, side, slots, channels), jnp.bfloat16),
            pltpu.VMEM(conv_weight.shape, jnp.bfloat16),
            pltpu.VMEM((channels // LANES, EDGE * rows, LANES), jnp.float32),
            pltpu.VMEM((6, slots), jnp.int32),
            pltpu.VMEM(occupancy.shape, jnp.int32),
            pltpu.VMEM((1, channels), jnp.float32),
            pltpu.VMEM((1, channels), jnp.float32),
            pltpu.SMEM(plan.shape, jnp.int32),
            pltpu.SemaphoreType.DMA((8,)),
        ],
        compiler_params=params(12),
        cost_estimate=cost(0, 1000),
    )(
        near(cube),
        near(from_core),
        near(from_next),
        *map(near, (own, other)),
        far(neighbors.T),
        far(occupancy),
        far(conv_weight),
        far(norm_scale[None]),
        far(norm_shift[None]),
        far(plan),
        parts[0],
        *map(near, early),
    )

    return pl.pallas_call(
        functools.partial(finish_kernel, room, planes),
        out_shape=[
            jax.ShapeDtypeStruct((slots, VOX, channels), jnp.bfloat16),
            blocks(slots + 1, VOX, channels),
        ],
        in_specs=[HBM, VMEM, VMEM, VMEM] + [VMEM] * planes,
        out_specs=[HBM, VMEM],
        input_output_aliases={3: 1},
        scratch_shapes=[
            blocks(slots, VOX, channels),
            pltpu.SMEM(plan.shape, jnp.int32),
            pltpu.SemaphoreType.DMA((1 + -(-slots // 4),)),
        ],
        compiler_params=params(4),
        cost_estimate=cost(0, 1000),
    )(far(plan), *map(near, (hidden, prev_taps, moved, *late)))[0]


def solution(mesh):
    rows = ("grp", "blk")
    in_specs = (
        P(rows, None, None),
        P(rows, None),
        P(rows, None),
        P(rows, None, None),
        P(rows, None),
        P(rows),
        P(),
        P(),
        P(),
        P(),
    )
    return jax.shard_map(
        per_device, mesh=mesh, in_specs=in_specs, out_specs=P(rows, None, None), check_vma=False
    )
```

```python
import functools

import jax
import jax.numpy as jnp
from jax import lax
from jax.experimental import pallas as pl
from jax.experimental.pallas import tpu as pltpu
from jax.sharding import PartitionSpec as P

EDGE = 4
LAYER = EDGE * EDGE
VOX = EDGE * LAYER
PLANE = 4
LANES = 128
HBM = pl.BlockSpec(memory_space=pl.ANY)
VMEM = pl.BlockSpec(memory_space=pltpu.VMEM)
SMEM = pl.BlockSpec(memory_space=pltpu.SMEM)


def near(array):
    return pltpu.with_memory_space_constraint(array, pltpu.VMEM)


def far(array):
    return pltpu.with_memory_space_constraint(array, pltpu.HBM)


def cost(flops, moved):
    return pl.CostEstimate(flops=flops, bytes_accessed=moved, transcendentals=0)


def occupied(occ, layer, channels):
    slots = occ.shape[0]
    shape = (LAYER, slots, VOX)
    voxel = lax.broadcasted_iota(jnp.int32, shape, 0) + layer * LAYER
    column = lax.broadcasted_iota(jnp.int32, shape, 2)
    picked = jnp.where(voxel == column, jnp.broadcast_to(occ[None], shape), 0.0)
    picked = picked.astype(jnp.bfloat16).reshape(LAYER * slots, VOX)
    ones = jnp.ones((VOX, channels), jnp.bfloat16)
    return jnp.dot(picked, ones, preferred_element_type=jnp.float32)


def params(mib):
    return pltpu.CompilerParams(vmem_limit_bytes=mib * 1024 * 1024)


def start_all(pairs, sems):
    copies = [pltpu.make_async_copy(src, dst, sems.at[i]) for i, (src, dst) in enumerate(pairs)]
    for copy in copies:
        copy.start()
    return copies


def prepare_kernel(
    features, occupancy, previous, prev_weight, after, after2,
    cube, core, next_, own, prev_taps, values_in, occ_in, sems,
):
    slots, _, channels = features.shape
    rows = LAYER * slots
    copies = start_all(((features, values_in), (occupancy, occ_in), (previous, own), (prev_weight, prev_taps)), sems)
    row = lax.broadcasted_iota(jnp.int32, (rows, rows), 0)
    column = lax.broadcasted_iota(jnp.int32, (rows, rows), 1)
    swap = (row // slots == column % LAYER) & (row % slots == column // LAYER)
    swap = jnp.where(swap, 1.0, 0.0).astype(jnp.bfloat16)
    even = lax.rem(lax.axis_index("blk"), 2) == 0
    copies[1].wait()
    occ = occ_in[...].astype(jnp.float32)
    copies[0].wait()
    for layer in range(EDGE):
        span = pl.ds(layer * LAYER, LAYER)
        values = values_in[:, span, :].reshape(rows, channels)
        turned = jnp.dot(swap, values, preferred_element_type=jnp.float32)
        turned = turned * occupied(occ, layer, channels)
        cube[span] = turned.astype(jnp.bfloat16).reshape(LAYER, slots, channels)
    first, last = pl.ds(0, LAYER), pl.ds(VOX - LAYER, LAYER)

    @pl.when(even)
    def _():
        core[...] = cube[last]
        next_[...] = cube[first]

    @pl.when(jnp.logical_not(even))
    def _():
        core[...] = cube[first]
        next_[...] = cube[last]

    copies[2].wait()
    copies[3].wait()


def conv_kernel(
    room, steps, cube, core, next_, own, other, near_t, occupancy, weight, scale, shift, plan, after, *refs
):
    early = refs[:steps]
    hidden, moved, volume, taps, total, near_in, occ_in, scale_in, shift_in, plan_in, sems = refs[steps:]
    slots, channels = cube.shape[1], cube.shape[2]
    rows = LAYER * slots
    side = EDGE + 2
    copies = start_all(
        [(near_t, near_in), (occupancy, occ_in), (scale, scale_in), (shift, shift_in), (plan, plan_in)]
        + [(weight.at[pl.ds(9 * a, 9)], taps.at[pl.ds(9 * a, 9)]) for a in range(3)],
        sems,
    )
    even = lax.rem(lax.axis_index("blk"), 2) == 0
    volume[...] = jnp.zeros(volume.shape, volume.dtype)
    inner = pl.ds(1, EDGE)
    cells = cube[...].reshape(EDGE, EDGE, EDGE, slots, channels)
    volume[inner, inner, inner] = cells

    row = lax.broadcasted_iota(jnp.int32, (rows, rows), 0)
    column = lax.broadcasted_iota(jnp.int32, (rows, rows), 1)
    same_place = row // slots == column // slots
    slot_of = (column % slots).astype(jnp.float32)
    spread = lax.broadcasted_iota(jnp.int32, (rows, slots), 0) % slots
    spread = spread == lax.broadcasted_iota(jnp.int32, (rows, slots), 1)
    spread = jnp.where(spread, 1.0, 0.0).astype(jnp.bfloat16)
    for copy in copies[:5]:
        copy.wait()
    near_rows = lax.dot_general(
        spread,
        near_in[...].astype(jnp.float32).astype(jnp.bfloat16),
        (((1,), (1,)), ((), ())),
        preferred_element_type=jnp.float32,
    )

    for i in range(room):
        fill(moved.at[plan_in[i]], own, other, plan_in[2 * (steps + 1) * room + i])
        for k in range(steps):
            moved[plan_in[2 * (k + 1) * room + i]] = early[k][i]

    def gathered(face, layer):
        pick = same_place & (slot_of == near_rows[:, face : face + 1])
        pick = jnp.where(pick, 1.0, 0.0).astype(jnp.bfloat16)
        layer = layer.reshape(rows, channels)
        out = jnp.dot(pick, layer, preferred_element_type=jnp.float32).astype(jnp.bfloat16)
        return out.reshape(EDGE, EDGE, slots, channels)

    @pl.when(even)
    def _():
        volume[0, inner, inner] = gathered(0, next_[...])
        volume[EDGE + 1, inner, inner] = gathered(1, core[...])

    @pl.when(jnp.logical_not(even))
    def _():
        volume[0, inner, inner] = gathered(0, core[...])
        volume[EDGE + 1, inner, inner] = gathered(1, next_[...])

    last = EDGE - 1
    volume[inner, 0, inner] = gathered(2, cells[:, last])
    volume[inner, EDGE + 1, inner] = gathered(3, cells[:, 0])
    volume[inner, inner, 0] = gathered(4, cells[:, :, last])
    volume[inner, inner, EDGE + 1] = gathered(5, cells[:, :, 0])

    occ = occ_in[...].astype(jnp.float32)
    for a in range(3):
        copies[5 + a].wait()
        for x in range(EDGE):
            windows = [
                volume[x + a, pl.ds(b, EDGE), pl.ds(c, EDGE)].reshape(rows, channels)
                for b in range(3)
                for c in range(3)
            ]
            joined = jnp.concatenate(windows, axis=1)
            kernel = taps[pl.ds(9 * a, 9)].reshape(9 * channels, channels)
            part = jnp.dot(joined, kernel, preferred_element_type=jnp.float32)
            span = pl.ds(x * rows, rows)
            if a == 2:
                full = occupied(occ, x, LANES)
            for h in range(channels // LANES):
                lanes = slice(h * LANES, (h + 1) * LANES)
                if a == 0:
                    total[h, span] = part[:, lanes]
                elif a == 1:
                    total[h, span] += part[:, lanes]
                else:
                    out = (total[h, span] + part[:, lanes]) * scale_in[:, lanes] + shift_in[:, lanes]
                    total[h, span] = jnp.where(full > 0.5, jnp.maximum(out, 0.0), -1.0)
    for x in range(EDGE):
        for slot in range(slots):
            for h in range(channels // LANES):
                hidden[slot, pl.ds(x * LAYER, LAYER), pl.ds(h * LANES, LANES)] = total[
                    h, pl.ds(x * rows + slot, LAYER, stride=slots), :
                ]


def ask_kernel(room, planes, owner_in, slot_in, *refs):
    steps = planes - 1
    asks, plan = refs[:steps], refs[steps]
    old_owner, old_slot, queue, used, sems = refs[steps + 1 :]
    slots = old_slot.shape[0]
    width = 2 * room
    copies = start_all(((owner_in, old_owner), (slot_in, old_slot)), sems)
    me = lax.axis_index("blk")

    def clear(i, _):
        queue[i] = 0
        plan[i] = slots
        return 0

    lax.fori_loop(0, planes * width, clear, 0)
    for k in range(2 * planes):
        used[k] = 0
    for copy in copies:
        copy.wait()

    def place(s, _):
        away = lax.bitwise_xor(old_owner[s], me)
        chip = away // 2
        n = used[chip]
        used[chip] = n + 1
        at = chip * room + n
        queue[at] = lax.bitwise_and(away, 1) * slots + old_slot[s]
        plan[at] = s
        return 0

    lax.fori_loop(0, slots, place, 0)
    for i in range(width):
        plan[planes * width + i] = queue[i]
        for k in range(1, planes):
            asks[k - 1][i] = queue[k * width + i]


def fill(out, own, other, block):
    slots = own.shape[0]

    @pl.when(block < slots)
    def _():
        out[...] = own[block]

    @pl.when(block >= slots)
    def _():
        out[...] = other[block - slots]


def same_kernel(room, steps, plan, own, other, *refs):
    asks, outs = refs[:steps], refs[steps : 2 * steps]
    lists, asks_in, plan_in, sems = refs[2 * steps :]
    copies = start_all([(asks[k], asks_in.at[k]) for k in range(steps)] + [(plan, plan_in)], sems)
    for k in range(steps):
        copies[k].wait()
        for i in range(room):
            fill(outs[k].at[i], own, other, asks_in[k, i])
            lists[(k + 1) * room + i] = asks_in[k, room + i]
    copies[steps].wait()
    for i in range(room):
        lists[i] = plan_in[2 * (steps + 1) * room + room + i]


def cross_kernel(room, planes, lists, own, other, after, *refs):
    outs, lists_in, sems = refs[:planes], *refs[planes:]
    copies = start_all(((lists, lists_in),), sems)
    copies[0].wait()
    for k in range(planes):
        for i in range(room):
            fill(outs[k].at[i], own, other, lists_in[k * room + i])


def finish_kernel(room, planes, plan, hidden, weight_in, gathered, *refs):
    cross = refs[:planes]
    out, moved, merged, plan_in, sems = refs[planes:]
    slots = out.shape[0]
    copies = start_all(((plan, plan_in),), sems)
    copies[0].wait()
    for k in range(planes):
        for i in range(room):
            moved[plan_in[(2 * k + 1) * room + i]] = cross[k][i]
    group = min(4, slots)
    sent = []
    for j, g in enumerate(range(0, slots, group)):
        span = pl.ds(g, group)
        values = moved[span].reshape(group * VOX, moved.shape[2])
        projected = jnp.dot(values, weight_in[...], preferred_element_type=jnp.float32)
        projected = projected.astype(jnp.bfloat16).astype(jnp.float32)
        base = hidden[span].reshape(group * VOX, hidden.shape[2])
        done = jnp.where(base < 0.0, 0.0, base + projected)
        merged[span] = done.astype(out.dtype).reshape(group, VOX, out.shape[2])
        sent.append(pltpu.make_async_copy(merged.at[span], out.at[span], sems.at[1 + j]))
        sent[-1].start()
    for copy in sent:
        copy.wait()


def per_device(
    features,
    occupancy,
    neighbors,
    previous,
    old_owner,
    old_slot,
    conv_weight,
    norm_scale,
    norm_shift,
    prev_weight,
):
    slots, _, channels = features.shape
    rows = LAYER * slots
    count = lax.axis_size("blk")
    planes = count // PLANE
    steps = planes - 1
    room = 2 * max(2, 2 * slots // count)
    width = 2 * room

    def swap(array, flip):
        return lax.ppermute(array, "blk", [(i, i ^ flip) for i in range(count)])

    def ints(*shape):
        return jax.ShapeDtypeStruct(shape, jnp.int32)

    def blocks(*shape):
        return pltpu.VMEM(shape, jnp.bfloat16)

    other = swap(previous, 1)

    *asks, plan = pl.pallas_call(
        functools.partial(ask_kernel, room, planes),
        out_shape=[ints(width)] * steps + [ints((planes + 1) * width)],
        in_specs=[HBM] * 2,
        out_specs=[SMEM] * (steps + 1),
        scratch_shapes=[
            pltpu.SMEM((slots,), jnp.int32),
            pltpu.SMEM((slots,), jnp.int32),
            pltpu.SMEM((planes * width,), jnp.int32),
            pltpu.SMEM((2 * planes,), jnp.int32),
            pltpu.SemaphoreType.DMA((2,)),
        ],
        compiler_params=params(1),
        cost_estimate=cost(0, 1000),
    )(far(old_owner.reshape(slots)), far(old_slot))
    asked = [swap(ask, PLANE * k) for k, ask in enumerate(asks, 1)]

    cube, to_core, to_next, own, prev_taps = pl.pallas_call(
        prepare_kernel,
        out_shape=[
            blocks(VOX, slots, channels),
            blocks(LAYER, slots, channels),
            blocks(LAYER, slots, channels),
            blocks(*previous.shape),
            blocks(*prev_weight.shape),
        ],
        in_specs=[HBM] * 6,
        out_specs=[VMEM] * 5,
        scratch_shapes=[
            pltpu.VMEM(features.shape, features.dtype),
            pltpu.VMEM(occupancy.shape, occupancy.dtype),
            pltpu.SemaphoreType.DMA((4,)),
        ],
        compiler_params=params(4),
        cost_estimate=cost(0, 1000),
    )(far(features), far(occupancy), far(previous), far(prev_weight), plan, other)
    from_core = swap(to_core, 1)
    from_next = lax.ppermute(
        to_next,
        "blk",
        [pair for i in range(1, count - 1, 2) for pair in ((i, i + 1), (i + 1, i))],
    )

    *parts, lists = pl.pallas_call(
        functools.partial(same_kernel, room, steps),
        out_shape=[blocks(room, VOX, channels)] * steps + [ints(planes * room)],
        in_specs=[VMEM] * (3 + steps),
        out_specs=[VMEM] * steps + [SMEM],
        scratch_shapes=[
            pltpu.SMEM((steps, width), jnp.int32),
            pltpu.SMEM(plan.shape, jnp.int32),
            pltpu.SemaphoreType.DMA((steps + 1,)),
        ],
        compiler_params=params(1),
        cost_estimate=cost(0, 1000),
    )(*map(near, (plan, own, other, *asked)))
    early = {k: swap(parts[k - 1], PLANE * k) for k in sorted(range(1, planes), key=lambda k: k < 2)}
    early = [early[k] for k in range(1, planes)]
    lists = swap(lists, 2)

    parts = pl.pallas_call(
        functools.partial(cross_kernel, room, planes),
        out_shape=[blocks(room, VOX, channels)] * planes,
        in_specs=[VMEM] * 3 + [HBM],
        out_specs=[VMEM] * planes,
        scratch_shapes=[pltpu.SMEM((planes * room,), jnp.int32), pltpu.SemaphoreType.DMA((1,))],
        compiler_params=params(1),
        cost_estimate=cost(0, 1000),
    )(near(lists), near(own), near(other), from_next)
    late = {k: swap(parts[k], PLANE * k + 2) for k in sorted(range(planes), key=lambda k: k < 2)}
    late = [late[k] for k in range(planes)]

    side = EDGE + 2
    hidden, moved = pl.pallas_call(
        functools.partial(conv_kernel, room, steps),
        out_shape=[
            pltpu.VMEM((slots, VOX, channels), jnp.float32),
            blocks(slots + 1, VOX, channels),
        ],
        in_specs=[VMEM] * 5 + [HBM] * 5 + [VMEM, HBM] + [VMEM] * steps,
        out_specs=[VMEM] * 2,
        scratch_shapes=[
            pltpu.VMEM((side, side, side, slots, channels), jnp.bfloat16),
            pltpu.VMEM(conv_weight.shape, jnp.bfloat16),
            pltpu.VMEM((channels // LANES, EDGE * rows, LANES), jnp.float32),
            pltpu.VMEM((6, slots), jnp.int32),
            pltpu.VMEM(occupancy.shape, jnp.int32),
            pltpu.VMEM((1, channels), jnp.float32),
            pltpu.VMEM((1, channels), jnp.float32),
            pltpu.SMEM(plan.shape, jnp.int32),
            pltpu.SemaphoreType.DMA((8,)),
        ],
        compiler_params=params(12),
        cost_estimate=cost(0, 1000),
    )(
        near(cube),
        near(from_core),
        near(from_next),
        *map(near, (own, other)),
        far(neighbors.T),
        far(occupancy),
        far(conv_weight),
        far(norm_scale[None]),
        far(norm_shift[None]),
        near(plan),
        parts[0],
        *map(near, early),
    )

    return pl.pallas_call(
        functools.partial(finish_kernel, room, planes),
        out_shape=[
            jax.ShapeDtypeStruct((slots, VOX, channels), jnp.bfloat16),
            blocks(slots + 1, VOX, channels),
        ],
        in_specs=[VMEM] * (4 + planes),
        out_specs=[HBM, VMEM],
        input_output_aliases={3: 1},
        scratch_shapes=[
            blocks(slots, VOX, channels),
            pltpu.SMEM(plan.shape, jnp.int32),
            pltpu.SemaphoreType.DMA((1 + -(-slots // 4),)),
        ],
        compiler_params=params(4),
        cost_estimate=cost(0, 1000),
    )(*map(near, (plan, hidden, prev_taps, moved, *late)))[0]


def solution(mesh):
    rows = ("grp", "blk")
    in_specs = (
        P(rows, None, None),
        P(rows, None),
        P(rows, None),
        P(rows, None, None),
        P(rows, None),
        P(rows),
        P(),
        P(),
        P(),
        P(),
    )
    return jax.shard_map(
        per_device, mesh=mesh, in_specs=in_specs, out_specs=P(rows, None, None), check_vma=False
    )
```
